32 devices in a mesh: ctx: 16 (over z, y, core), ch: 2 (over x).
Axes of the slice: x: 2, y: 2, z: 4, core: 2. Of those that a mesh axis runs over, the one named last changes fastest.
Arguments:
- mr_query: bfloat16 [4096, 4096], P('ch', 'ctx'), may hold values from -6 to 6
- mr_key: bfloat16 [4096, 4096], P('ch', 'ctx'), may hold values from -6 to 6
- mr_value: bfloat16 [4096, 4096], P('ch', 'ctx'), may hold values from -6 to 6
- mr_filter: float32 [4096, 128], P('ch'), may hold values from -0.5 to 0.5
- proj_weight: bfloat16 [4096, 4096], P('ch'), may hold values from -0.09375 to 0.09375
- li_query: bfloat16 [4096, 4096], P('ch', 'ctx'), may hold values from -6 to 6
- li_key: bfloat16 [4096, 4096], P('ch', 'ctx'), may hold values from -6 to 6
- li_filter: bfloat16 [4096, 4096], P('ch', 'ctx'), may hold values from -0.09375 to 0.09375
- li_skip: float32 [4096], P('ch'), may hold values from 0.5 to 1.5
Outputs:
- gated_out: bfloat16 [4096, 4096], P('ch', 'ctx')
The draws below stay inside these ranges and needn't reach their ends.
All inputs are finite; a program needn't handle non-finite values.
Results may differ from the reference program's by a relative error of at most 0.0066.
Values may be sent and summed in bfloat16 or wider, within the bound.
No kernel may reach another device: no remote copies, remote signals or barrier semaphores. Data moves between devices by JAX's collectives and lax.ppermute only.
A program may use at most 128 MiB of HBM per device.

```python
import jax
import jax.numpy as jnp
from jax import lax

D = 4096
TAPS = 128
TOKENS = 4096


def level_of(own_key, extent, split, low, top_value):
    def one(position, parts):
        heights = jax.random.uniform(jax.random.fold_in(jax.random.fold_in(own_key, 6), position), (parts,), jnp.float32, low / len(split), top_value / len(split))
        return jnp.repeat(jnp.exp(heights), extent[position] // parts).reshape((-1,) + (1,) * (len(extent) - position - 1))

    gain = one(*split[0])
    for cut in split[1:]:
        gain = gain * one(*cut)
    return gain


def centred(stream_key, dims, spread, reach, shards=(), kind=jnp.bfloat16):
    entries = spread * jax.random.normal(stream_key, dims, jnp.float32)
    if shards:
        entries = entries * level_of(stream_key, dims, shards, -0.22, 0.18)
    return jnp.clip(entries, -reach, reach).astype(kind)


def setup_inputs(seed: int = 0) -> dict:
    arg_keys = jax.random.split(jax.random.key(seed), 10)
    return {
        "mr_query": centred(arg_keys[0], (D, TOKENS), 1.0, 6.0, ((0, 2), (1, 16))),
        "mr_key": centred(arg_keys[1], (D, TOKENS), 1.0, 6.0, ((0, 2), (1, 16))),
        "mr_value": centred(arg_keys[2], (D, TOKENS), 1.0, 6.0, ((0, 2), (1, 16))),
        "mr_filter": centred(arg_keys[3], (D, TAPS), TAPS ** -0.5, 0.5, ((0, 2),), jnp.float32),
        "proj_weight": centred(arg_keys[4], (D, D), D ** -0.5, 0.09375, ((0, 2),)),
        "li_query": centred(arg_keys[5], (D, TOKENS), 1.0, 6.0, ((0, 2), (1, 16))),
        "li_key": centred(arg_keys[6], (D, TOKENS), 1.0, 6.0, ((0, 2), (1, 16))),
        "li_filter": centred(arg_keys[7], (D, TOKENS), TOKENS ** -0.5, 0.09375, ((0, 2), (1, 16))),
        "li_skip": jnp.clip(0.5 + 1.0 * jax.random.uniform(arg_keys[8], (D,), jnp.float32) ** level_of(arg_keys[8], (D,), ((0, 2),), -0.2, 0.2), 0.5, 1.5),
    }


def round_half(tensor):
    return lax.optimization_barrier(tensor.astype(jnp.bfloat16))


def causal_taps(signal, taps):
    tap_count = taps.shape[1]
    seq_length = signal.shape[1]
    blocks = signal.shape[0] // 128
    shaped = signal.reshape(blocks, 128, seq_length)
    shaped_taps = taps.astype(signal.dtype).reshape(blocks, 128, tap_count)

    def single_block(block_pair):
        block_signal = block_pair[0]
        block_taps = block_pair[1]
        padded = jnp.pad(block_signal, ((0, 0), (tap_count - 1, 0)))

        def add_tap(index, total):
            start = (tap_count - 1 - index).astype(jnp.int32)
            piece = lax.dynamic_slice_in_dim(padded, start, seq_length, 1)
            weight = lax.dynamic_slice_in_dim(block_taps, index.astype(jnp.int32), 1, 1)
            return total + weight * piece

        return lax.fori_loop(jnp.int32(0), jnp.int32(tap_count), add_tap, jnp.zeros(block_signal.shape, block_signal.dtype))

    result = lax.map(single_block, (shaped, shaped_taps))
    return result.reshape(blocks * 128, seq_length)


def long_reference(li_input, li_filter):
    seq_length = li_input.shape[1]
    blocks = li_input.shape[0] // 128
    signal = li_input.astype(jnp.float32).reshape(blocks, 128, seq_length)
    kernel = li_filter.astype(jnp.float32).reshape(blocks, 128, seq_length)

    def single_block(blocks_pair):
        spectra = jnp.fft.rfft(blocks_pair[0], n=2 * seq_length, axis=1) * jnp.fft.rfft(blocks_pair[1], n=2 * seq_length, axis=1)
        return jnp.fft.irfft(spectra, n=2 * seq_length, axis=1)[:, :seq_length].astype(jnp.float32)

    result = lax.map(single_block, (signal, kernel))
    return result.reshape(blocks * 128, seq_length)


def reference(mr_query, mr_key, mr_value, mr_filter, proj_weight, li_query, li_key, li_filter, li_skip):
    mr_input = round_half(mr_key.astype(jnp.float32) * mr_value.astype(jnp.float32))
    mr_mixed = causal_taps(mr_input.astype(jnp.float32), mr_filter)
    mr_output = (mr_query.astype(jnp.float32) * mr_mixed).astype(jnp.bfloat16)
    values = jnp.dot(proj_weight, mr_output, preferred_element_type=jnp.float32)
    li_input = round_half(li_key.astype(jnp.float32) * values)
    long_part = round_half(long_reference(li_input, li_filter))
    gated_out = li_query.astype(jnp.float32) * (long_part.astype(jnp.float32) + li_skip[:, None] * li_input.astype(jnp.float32))
    return gated_out.astype(jnp.bfloat16)
```

```python
import functools
import math

import jax
import jax.numpy as jnp
import numpy as np
from jax import lax
from jax.experimental import pallas as pl
from jax.experimental.pallas import tpu as pltpu
from jax.sharding import PartitionSpec as P

F32 = jnp.float32
BF16 = jnp.bfloat16
MIB = 1 << 20


def split_table(table):
    high = table.astype(np.float32).astype(BF16)
    low = (table - high.astype(np.float64)).astype(np.float32).astype(BF16)
    return np.asarray(high), np.asarray(low)


def split_value(value):
    high = value.astype(BF16)
    return high, (value - high.astype(F32)).astype(BF16)


def dot(left, right):
    return jnp.dot(left, right, preferred_element_type=F32)


def short_tables(size):
    half = size // 2
    time = np.arange(size)[:, None]
    freq = np.arange(half)[None, :]
    angle = 2.0 * np.pi * (time * freq % size) / size
    forward = np.concatenate([np.cos(angle), -np.sin(angle)], axis=1)
    forward[:, half] = np.where(np.arange(size) % 2 == 0, 1.0, -1.0)
    inverse = forward.T * (2.0 / size)
    inverse[0] /= 2.0
    inverse[half] /= 2.0
    return split_table(forward) + split_table(inverse[:, half:])


def short_filter(window, taps, query, fwd_hi, fwd_lo, inv_hi, inv_lo):
    half = taps.shape[1]
    spec = dot(window, fwd_hi) + dot(window, fwd_lo)
    taps_hi, taps_lo = split_value(taps)
    resp = dot(taps_hi, fwd_hi[:half]) + dot(taps_lo, fwd_hi[:half]) + dot(taps_hi, fwd_lo[:half])
    first = lax.broadcasted_iota(jnp.int32, (taps.shape[0], half), 1) == 0
    resp_re, resp_im = resp[:, :half], resp[:, half:]
    cross = jnp.where(first, 0.0, resp_im)
    own = jnp.where(first, resp_im, resp_re)
    spec_re, spec_im = spec[:, :half], spec[:, half:]
    prod = jnp.concatenate(
        [spec_re * resp_re - spec_im * cross, spec_re * cross + spec_im * own], axis=1
    )
    prod_hi, prod_lo = split_value(prod)
    mixed = dot(prod_hi, inv_hi) + dot(prod_lo, inv_hi) + dot(prod_hi, inv_lo)
    return (query.astype(F32) * mixed).astype(BF16)


def gate_input(key, value):
    return (key.astype(F32) * value.astype(F32)).astype(BF16)


def late_kernel(key, value, query, taps, fwd_hi, fwd_lo, inv_hi, inv_lo, out):
    window = gate_input(key[...], value[...])
    out[...] = short_filter(
        window, taps[...], query[...], fwd_hi[...], fwd_lo[...], inv_hi[...], inv_lo[...]
    )


def early_kernel(border, key, value, query, taps, fwd_hi, fwd_lo, inv_hi, inv_lo, out):
    window = jnp.concatenate([border[...], gate_input(key[...], value[...])], axis=1)
    out[...] = short_filter(
        window, taps[...], query[...], fwd_hi[...], fwd_lo[...], inv_hi[...], inv_lo[...]
    )


def whole_spec(array):
    return pl.BlockSpec(array.shape, lambda *_: (0,) * array.ndim)


def short_conv(border, key, value, query, taps, tables):
    rows, tokens = key.shape
    half = tokens // 2
    block = min(rows, 512)
    table_specs = [whole_spec(t) for t in tables]
    full = pl.BlockSpec((block, tokens), lambda i: (i, 0))
    left = pl.BlockSpec((block, half), lambda i: (i, 0))
    right = pl.BlockSpec((block, half), lambda i: (i, 1))
    if border is None:
        body, specs, args = late_kernel, [full, full, right, left], (key, value, query, taps)
    else:
        body, specs = early_kernel, [left, left, left, left, left]
        args = (border, key, value, query, taps)
    return pl.pallas_call(
        body,
        grid=(rows // block,),
        in_specs=specs + table_specs,
        out_specs=left,
        out_shape=jax.ShapeDtypeStruct((rows, half), BF16),
        compiler_params=pltpu.CompilerParams(vmem_limit_bytes=32 * MIB),
        cost_estimate=pl.CostEstimate(
            flops=10 * rows * tokens * tokens, bytes_accessed=8 * rows * tokens, transcendentals=0
        ),
    )(*args, *tables)


def own_kernel(which, weight, late, early, out):
    del which
    out[...] = dot(weight[...], jnp.concatenate([early[...], late[...]], axis=1))


def other_kernel(which, weight, late, early, total, key, out):
    del which
    values = total[...] + dot(weight[...], jnp.concatenate([early[...], late[...]], axis=1))
    out[...] = (key[...].astype(F32) * values).astype(BF16)


def project(which, weight, late, early, total=None, key=None):
    rows, depth = weight.shape[0], late.shape[0]
    half = late.shape[1]
    block = min(rows, 256)
    moving = pl.BlockSpec((block, 2 * half), lambda i, w: (i, 0))
    specs = [
        pl.BlockSpec((block, depth), lambda i, w: (i, w[0])),
        pl.BlockSpec((depth, half), lambda i, w: (0, 0)),
        pl.BlockSpec((depth, half), lambda i, w: (0, 0)),
    ]
    args = [weight, late, early]
    if total is None:
        body, dtype = own_kernel, F32
    else:
        body, dtype = other_kernel, BF16
        specs += [moving, moving]
        args += [total, key]
    return pl.pallas_call(
        body,
        grid_spec=pltpu.PrefetchScalarGridSpec(
            num_scalar_prefetch=1, grid=(rows // block,), in_specs=specs, out_specs=moving
        ),
        out_shape=jax.ShapeDtypeStruct((rows, 2 * half), dtype),
        compiler_params=pltpu.CompilerParams(vmem_limit_bytes=32 * MIB),
        cost_estimate=pl.CostEstimate(
            flops=4 * rows * depth * half, bytes_accessed=2 * rows * depth, transcendentals=0
        ),
    )(which, *args)


def turn(value, num, den):
    num %= den
    if num < 0:
        num += den
    re, im = value
    if num == 0:
        return value
    if 4 * num == den:
        return (im, -re)
    if 2 * num == den:
        return (-re, -im)
    if 4 * num == 3 * den:
        return (-im, re)
    cos = math.cos(2.0 * math.pi * num / den)
    sin = math.sin(2.0 * math.pi * num / den)
    if 8 * num % den == 0:
        size = math.sqrt(0.5)
        cos, sin = (1 if cos > 0 else -1), (1 if sin > 0 else -1)
        first = re + im if cos == sin else re - im
        second = im - re if cos == sin else im + re
        if cos > 0:
            return (size * first, size * second)
        return ((-size) * first, (-size) * second)
    return (cos * re + sin * im, cos * im - sin * re)


def add(a, b):
    return (a[0] + b[0], a[1] + b[1])


def sub(a, b):
    return (a[0] - b[0], a[1] - b[1])


def dft(values, sign):
    size = len(values)
    if size == 1:
        return values
    half = size // 2
    even = dft([add(values[n], values[n + half]) for n in range(half)], sign)
    odd = dft(
        [turn(sub(values[n], values[n + half]), sign * n, size) for n in range(half)], sign
    )
    out = []
    for n in range(half):
        out += [even[n], odd[n]]
    return out


def odd_part(values, size):
    half = len(values) // 2
    shaped = [turn((values[n], -values[n + half]), n, size) for n in range(half)]
    found = {}
    for r, value in enumerate(dft(shaped, 1)):
        k = 4 * r + 1
        if k < size // 2:
            found[k] = value
        else:
            found[size - k] = (value[0], -value[1])
    return found


def real_dft(values):
    size = len(values)
    if size == 2:
        return {0: (values[0] + values[1], None), 1: (values[0] - values[1], None)}
    half = size // 2
    found = {
        2 * k: v
        for k, v in real_dft([values[n] + values[n + half] for n in range(half)]).items()
    }
    found.update(odd_part([values[n] - values[n + half] for n in range(half)], size))
    return found


def padded_dft(values):
    found = {2 * k: v for k, v in real_dft(values).items()}
    found.update(odd_part(values, 2 * len(values)))
    return found


def odd_back(found, size):
    quarter = size // 4
    terms = []
    for r in range(quarter):
        k = 4 * r + 1
        if k < size // 2:
            terms.append(found[k])
        else:
            value = found[size - k]
            terms.append((value[0], -value[1]))
    back = [turn(value, -n, size) for n, value in enumerate(dft(terms, -1))]
    return [v[0] for v in back] + [-v[1] for v in back]


def real_back(found, size):
    if size == 2:
        return [found[0][0] + found[1][0], found[0][0] - found[1][0]]
    half = size // 2
    even = real_back({k // 2: v for k, v in found.items() if k % 2 == 0}, half)
    odd = odd_back(found, size)
    return [even[n] + odd[n] for n in range(half)] + [even[n] - odd[n] for n in range(half)]


def padded_back(found, size):
    even = real_back({k // 2: v for k, v in found.items() if k % 2 == 0}, size)
    odd = odd_back(found, 2 * size)
    return [e + o for e, o in zip(even, odd)]


def long_tables(slabs, tokens):
    full = 2 * slabs * tokens
    token = np.arange(tokens)
    angle = 2.0 * np.pi * (np.arange(slabs + 1)[:, None] * token[None, :] % full) / full
    cos, sin = np.cos(angle), -np.sin(angle)
    back_scale = np.full((slabs + 1, 1), 2.0 / full)
    back_scale[0] = back_scale[slabs] = 1.0 / full
    inner = 2.0 * np.pi * (token[:, None] * token[None, :] % tokens) / tokens
    re, im = np.cos(inner), -np.sin(inner)
    forward = np.block([[re, im], [-im, re]])
    inverse = np.block([[re, -im], [im, re]])
    turns = [t.astype(np.float32) for t in (cos, sin, cos * back_scale, -sin * back_scale)]
    return turns, split_table(forward), split_table(inverse)


LANES = 128
SUBS = 16


def forward_slabs(source, turn_re, turn_im, high, low):
    slabs, rows, tokens = source.shape
    lanes = min(tokens, LANES)
    subs = min(rows, SUBS)
    for lane in range(0, tokens, lanes):

        def tile(step, carry, lane=lane):
            at = pl.ds(pl.multiple_of(step * subs, subs), subs)
            values = [source[j, at, lane : lane + lanes].astype(F32) for j in range(slabs)]
            for k, (re, im) in padded_dft(values).items():
                cos = turn_re[k : k + 1, lane : lane + lanes]
                sin = turn_im[k : k + 1, lane : lane + lanes]
                if im is None:
                    out = (re * cos, re * sin)
                else:
                    out = (re * cos - im * sin, re * sin + im * cos)
                for part, value in enumerate(out):
                    where = slice(part * tokens + lane, part * tokens + lane + lanes)
                    hi, lo = split_value(value)
                    high[k, at, where] = hi
                    low[k, at, where] = lo
            return carry

        lax.fori_loop(0, rows // subs, tile, 0)


def product3(high, low, table_hi, table_lo):
    a, b = high[...], low[...]
    shape = a.shape
    a = a.reshape(shape[0] * shape[1], shape[2])
    b = b.reshape(shape[0] * shape[1], shape[2])
    out = dot(a, table_hi[...]) + dot(b, table_hi[...]) + dot(a, table_lo[...])
    return out.reshape(shape[0], shape[1], -1)


def response_kernel(source, turn_re, turn_im, table_hi, table_lo, out, high, low):
    forward_slabs(source, turn_re, turn_im, high, low)
    out[...] = product3(high, low, table_hi, table_lo)


def convolve_kernel(
    source, response, turn_re, turn_im, back_re, back_im, fwd_hi, fwd_lo, inv_hi, inv_lo, out, high, low, spec
):
    slabs, rows, tokens = source.shape
    lanes = min(tokens, LANES)
    subs = min(rows, SUBS)
    forward_slabs(source, turn_re, turn_im, high, low)
    spec[...] = product3(high, low, fwd_hi, fwd_lo)

    def multiply(k, carry):
        sig_re, sig_im = spec[k, :, :tokens], spec[k, :, tokens:]
        res_re, res_im = response[k, :, :tokens], response[k, :, tokens:]
        for part, value in enumerate(
            (sig_re * res_re - sig_im * res_im, sig_re * res_im + sig_im * res_re)
        ):
            hi, lo = split_value(value)
            high[k, :, part * tokens : (part + 1) * tokens] = hi
            low[k, :, part * tokens : (part + 1) * tokens] = lo
        return carry

    lax.fori_loop(0, slabs + 1, multiply, 0)
    spec[...] = product3(high, low, inv_hi, inv_lo)
    for lane in range(0, tokens, lanes):

        def tile(step, carry, lane=lane):
            at = pl.ds(pl.multiple_of(step * subs, subs), subs)
            found = {}
            for k in range(slabs + 1):
                re = spec[k, at, lane : lane + lanes]
                im = spec[k, at, tokens + lane : tokens + lane + lanes]
                cos = back_re[k : k + 1, lane : lane + lanes]
                sin = back_im[k : k + 1, lane : lane + lanes]
                if k in (0, slabs):
                    found[k] = (re * cos - im * sin, None)
                else:
                    found[k] = (re * cos - im * sin, re * sin + im * cos)
            for j, value in enumerate(padded_back(found, slabs)):
                out[j, at, lane : lane + lanes] = value.astype(BF16)
            return carry

        lax.fori_loop(0, rows // subs, tile, 0)


def long_call(source, response, tables, start=0, count=None):
    slabs, rows, tokens = source.shape
    block = min(rows, 32)
    turns, forward, inverse = tables
    if response is None:
        body, given = response_kernel, [*turns[:2], *forward]
    else:
        body, given = convolve_kernel, [*turns, *forward, *inverse]
    data = pl.BlockSpec((slabs, block, tokens), lambda i: (0, i, 0))
    wide = pl.BlockSpec((slabs + 1, block, 2 * tokens), lambda i: (0, i, 0))
    scratch = [pltpu.VMEM((slabs + 1, block, 2 * tokens), t) for t in (BF16, BF16, F32)]
    flops = 12 * (slabs + 1) * rows * 4 * tokens * tokens
    if response is None:
        out_spec, out_shape, scratch = wide, ((slabs + 1, rows, 2 * tokens), F32), scratch[:2]
        args, specs = [source], [data]
    else:
        out_spec, out_shape = data, ((slabs, rows, tokens), BF16)
        args, specs = [source, response], [data, wide]
    return pl.pallas_call(
        body,
        grid=(rows // block,),
        in_specs=specs + [whole_spec(t) for t in given],
        out_specs=out_spec,
        out_shape=jax.ShapeDtypeStruct(*out_shape),
        scratch_shapes=scratch,
        compiler_params=pltpu.CompilerParams(vmem_limit_bytes=48 * MIB),
        cost_estimate=pl.CostEstimate(
            flops=flops, bytes_accessed=8 * (slabs + 1) * rows * tokens, transcendentals=0
        ),
    )(*args, *given)


def exchange(value, groups):
    rows, tokens = value.shape
    return lax.all_to_all(
        value.reshape(groups, rows // groups, tokens), "ctx", split_axis=0, concat_axis=0, tiled=True
    )


def on_device(
    mr_query, mr_key, mr_value, mr_filter, proj_weight, li_query, li_key, li_filter, li_skip
):
    rows, tokens = mr_key.shape
    half = tokens // 2
    groups = lax.axis_size("ctx")
    short = short_tables(tokens)
    tables = long_tables(groups, tokens)
    swap = [(0, 1), (1, 0)]

    border = gate_input(mr_key[:, half:], mr_value[:, half:])
    border = lax.ppermute(border, "ctx", [(i, i + 1) for i in range(groups - 1)])
    filter_part = exchange(li_filter, groups)

    late = short_conv(None, mr_key, mr_value, mr_query, mr_filter, short)
    other_late = lax.ppermute(late, "ch", swap)
    early = short_conv(border, mr_key, mr_value, mr_query, mr_filter, short)
    other_early = lax.ppermute(early, "ch", swap)

    me = lax.axis_index("ch").astype(jnp.int32).reshape(1)
    total = project(me, proj_weight, late, early)
    li_input = project(1 - me, proj_weight, other_late, other_early, total, li_key)

    response = long_call(filter_part, None, tables)
    long_part = long_call(exchange(li_input, groups), response, tables)
    long_local = exchange(long_part.reshape(rows, tokens), groups).reshape(rows, tokens)
    gated_out = li_query.astype(F32) * (
        long_local.astype(F32) + li_skip[:, None] * li_input.astype(F32)
    )
    return gated_out.astype(BF16)


def solution(mesh):
    in_specs = (
        P("ch", "ctx"),
        P("ch", "ctx"),
        P("ch", "ctx"),
        P("ch", None),
        P("ch", None),
        P("ch", "ctx"),
        P("ch", "ctx"),
        P("ch", "ctx"),
        P("ch"),
    )
    return jax.shard_map(
        on_device, mesh=mesh, in_specs=in_specs, out_specs=P("ch", "ctx"), check_vma=False
    )
```

```python
import functools
import math

import jax
import jax.numpy as jnp
import numpy as np
from jax import lax
from jax.experimental import pallas as pl
from jax.experimental.pallas import tpu as pltpu
from jax.sharding import PartitionSpec as P

F32 = jnp.float32
BF16 = jnp.bfloat16
MIB = 1 << 20


def split_table(table):
    high = table.astype(np.float32).astype(BF16)
    low = (table - high.astype(np.float64)).astype(np.float32).astype(BF16)
    return np.asarray(high), np.asarray(low)


def split_value(value):
    high = value.astype(BF16)
    return high, (value - high.astype(F32)).astype(BF16)


def dot(left, right):
    return jnp.dot(left, right, preferred_element_type=F32)


def short_tables(size):
    half = size // 2
    time = np.arange(size)[:, None]
    freq = np.arange(half)[None, :]
    angle = 2.0 * np.pi * (time * freq % size) / size
    forward = np.concatenate([np.cos(angle), -np.sin(angle)], axis=1)
    forward[:, half] = np.where(np.arange(size) % 2 == 0, 1.0, -1.0)
    inverse = forward.T * (2.0 / size)
    inverse[0] /= 2.0
    inverse[half] /= 2.0
    return (*split_table(forward), np.concatenate(split_table(inverse[:, half:]), axis=1))


def short_filter(window, taps, query, fwd_hi, fwd_lo, inverse):
    half = taps.shape[1]
    spec = dot(window, fwd_hi) + dot(window, fwd_lo)
    taps_hi, taps_lo = split_value(taps)
    doubled = jnp.concatenate([fwd_hi[:half], fwd_hi[:half]], axis=0)
    resp = dot(jnp.concatenate([taps_hi, taps_lo], axis=1), doubled) + dot(taps_hi, fwd_lo[:half])
    first = lax.broadcasted_iota(jnp.int32, (taps.shape[0], half), 1) == 0
    resp_re, resp_im = resp[:, :half], resp[:, half:]
    cross = jnp.where(first, 0.0, resp_im)
    own = jnp.where(first, resp_im, resp_re)
    spec_re, spec_im = spec[:, :half], spec[:, half:]
    prod = jnp.concatenate(
        [spec_re * resp_re - spec_im * cross, spec_re * cross + spec_im * own], axis=1
    )
    prod_hi, prod_lo = split_value(prod)
    both = dot(prod_hi, inverse)
    mixed = both[:, :half] + both[:, half:] + dot(prod_lo, inverse[:, :half])
    return (query.astype(F32) * mixed).astype(BF16)


def gate_input(key, value):
    return (key.astype(F32) * value.astype(F32)).astype(BF16)


def late_kernel(key, value, query, taps, fwd_hi, fwd_lo, inverse, out, border):
    window = gate_input(key[...], value[...])
    border[...] = window[:, query.shape[1] :]
    out[...] = short_filter(
        window, taps[...], query[...], fwd_hi[...], fwd_lo[...], inverse[...]
    )


def early_kernel(border, key, value, query, taps, fwd_hi, fwd_lo, inverse, out):
    window = jnp.concatenate([border[...], gate_input(key[...], value[...])], axis=1)
    out[...] = short_filter(
        window, taps[...], query[...], fwd_hi[...], fwd_lo[...], inverse[...]
    )


def whole_spec(array):
    return pl.BlockSpec(array.shape, lambda *_: (0,) * array.ndim)


def short_conv(border, key, value, query, taps, tables, block=1024):
    rows, tokens = key.shape
    half = tokens // 2
    block = min(rows, block)
    table_specs = [whole_spec(t) for t in tables]
    full = pl.BlockSpec((block, tokens), lambda i: (i, 0))
    left = pl.BlockSpec((block, half), lambda i: (i, 0))
    right = pl.BlockSpec((block, half), lambda i: (i, 1))
    if border is None:
        body, specs, outs = late_kernel, [full, full, right, left], 2
        args = (key, value, query, taps)
    else:
        body, specs, outs = early_kernel, [left, left, left, left, left], 1
        args = (border, key, value, query, taps)
    return pl.pallas_call(
        body,
        grid=(rows // block,),
        in_specs=specs + table_specs,
        out_specs=[left] * outs,
        out_shape=[jax.ShapeDtypeStruct((rows, half), BF16)] * outs,
        compiler_params=pltpu.CompilerParams(vmem_limit_bytes=60 * MIB),
        cost_estimate=pl.CostEstimate(
            flops=50 * rows * tokens * tokens, bytes_accessed=8 * rows * tokens, transcendentals=0
        ),
    )(*args, *tables)


def own_kernel(which, weight, late, early, late_out, early_out):
    del which
    half = late.shape[1]
    found = dot(weight[...], jnp.concatenate([late[...], early[...]], axis=1))

    @pl.when(pl.program_id(0) == 0)
    def _():
        late_out[...] = found[:, :half]
        early_out[...] = found[:, half:]

    @pl.when(pl.program_id(0) > 0)
    def _():
        late_out[...] += found[:, :half]
        early_out[...] += found[:, half:]


def other_kernel(pairs, which, weight, late, early, late_total, early_total, key, out, *refs):
    *pieces, sums = refs
    half = late.shape[1]
    found = dot(weight[...], jnp.concatenate([early[...], late[...]], axis=1))

    @pl.when(pl.program_id(0) == 0)
    def _():
        sums[:, :half] = early_total[...] + found[:, :half]
        sums[:, half:] = late_total[...] + found[:, half:]

    @pl.when(pl.program_id(0) > 0)
    def _():
        sums[...] += found

    @pl.when(pl.program_id(0) == pl.num_programs(0) - 1)
    def _():
        out[...] = (key[...].astype(F32) * sums[...]).astype(BF16)
        chip, core = which[1], which[2]
        for i, piece in enumerate(pieces):
            chunk, rel = divmod(i, pairs)
            rows = piece.shape[1]
            for slot in range(2):
                piece[slot] = out[chunk_rows(chip ^ rel, core ^ slot, chunk, rows), :]


def chunk_rows(chip, core, chunk, rows):
    start = ((chip * 2 + core) * CHUNKS + chunk) * rows
    return pl.ds(pl.multiple_of(start, rows), rows)


CHUNKS = 2
DEPTH = 1024


def project_own(which, weight, late, early):
    rows, (depth, half) = weight.shape[0], late.shape
    block = min(depth, DEPTH)
    steps = depth // block
    moving = pl.BlockSpec((block, half), lambda i, w: (i, 0))
    fixed = pl.BlockSpec((rows, half), lambda i, w: (0, 0))
    return pl.pallas_call(
        own_kernel,
        grid_spec=pltpu.PrefetchScalarGridSpec(
            num_scalar_prefetch=1,
            grid=(steps,),
            in_specs=[
                pl.BlockSpec((rows, block), lambda i, w: (0, w[0] * steps + i)),
                moving,
                moving,
            ],
            out_specs=[fixed, fixed],
        ),
        out_shape=[jax.ShapeDtypeStruct((rows, half), F32)] * 2,
        compiler_params=pltpu.CompilerParams(vmem_limit_bytes=56 * MIB),
        cost_estimate=pl.CostEstimate(
            flops=4 * rows * depth * half, bytes_accessed=2 * rows * depth, transcendentals=0
        ),
    )(which, weight, late, early)


def project_other(where, weight, late, early, late_total, early_total, key, pairs):
    rows, (depth, half) = weight.shape[0], late.shape
    block = min(depth, DEPTH)
    steps = depth // block
    moving = pl.BlockSpec((block, half), lambda i, w: (i, 0))
    fixed = pl.BlockSpec((rows, half), lambda i, w: (0, 0))
    full = pl.BlockSpec((rows, 2 * half), lambda i, w: (0, 0))
    shape = (2, rows // (2 * max(pairs, 1) * CHUNKS), 2 * half)
    piece = pl.BlockSpec(shape, lambda i, w: (0, 0, 0))
    return pl.pallas_call(
        functools.partial(other_kernel, pairs),
        grid_spec=pltpu.PrefetchScalarGridSpec(
            num_scalar_prefetch=1,
            grid=(steps,),
            in_specs=[
                pl.BlockSpec((rows, block), lambda i, w: (0, w[0] * steps + i)),
                moving,
                moving,
                fixed,
                fixed,
                full,
            ],
            out_specs=[full] + [piece] * (pairs * CHUNKS),
            scratch_shapes=[pltpu.VMEM((rows, 2 * half), F32)],
        ),
        out_shape=[jax.ShapeDtypeStruct((rows, 2 * half), BF16)]
        + [jax.ShapeDtypeStruct(shape, BF16)] * (pairs * CHUNKS),
        compiler_params=pltpu.CompilerParams(vmem_limit_bytes=60 * MIB),
        cost_estimate=pl.CostEstimate(
            flops=24 * rows * depth * half, bytes_accessed=2 * rows * depth, transcendentals=0
        ),
    )(where, weight, late, early, late_total, early_total, key)


def turn(value, num, den):
    num %= den
    if num < 0:
        num += den
    re, im = value
    if num == 0:
        return value
    if 4 * num == den:
        return (im, -re)
    if 2 * num == den:
        return (-re, -im)
    if 4 * num == 3 * den:
        return (-im, re)
    cos = math.cos(2.0 * math.pi * num / den)
    sin = math.sin(2.0 * math.pi * num / den)
    if 8 * num % den == 0:
        size = math.sqrt(0.5)
        cos, sin = (1 if cos > 0 else -1), (1 if sin > 0 else -1)
        first = re + im if cos == sin else re - im
        second = im - re if cos == sin else im + re
        if cos > 0:
            return (size * first, size * second)
        return ((-size) * first, (-size) * second)
    return (cos * re + sin * im, cos * im - sin * re)


def add(a, b):
    return (a[0] + b[0], a[1] + b[1])


def sub(a, b):
    return (a[0] - b[0], a[1] - b[1])


def dft(values, sign):
    size = len(values)
    if size == 1:
        return values
    half = size // 2
    even = dft([add(values[n], values[n + half]) for n in range(half)], sign)
    odd = dft(
        [turn(sub(values[n], values[n + half]), sign * n, size) for n in range(half)], sign
    )
    out = []
    for n in range(half):
        out += [even[n], odd[n]]
    return out


def odd_part(values, size):
    half = len(values) // 2
    shaped = [turn((values[n], -values[n + half]), n, size) for n in range(half)]
    found = {}
    for r, value in enumerate(dft(shaped, 1)):
        k = 4 * r + 1
        if k < size // 2:
            found[k] = value
        else:
            found[size - k] = (value[0], -value[1])
    return found


def real_dft(values):
    size = len(values)
    if size == 2:
        return {0: (values[0] + values[1], None), 1: (values[0] - values[1], None)}
    half = size // 2
    found = {
        2 * k: v
        for k, v in real_dft([values[n] + values[n + half] for n in range(half)]).items()
    }
    found.update(odd_part([values[n] - values[n + half] for n in range(half)], size))
    return found


def padded_dft(values):
    found = {2 * k: v for k, v in real_dft(values).items()}
    found.update(odd_part(values, 2 * len(values)))
    return found


def odd_back(found, size):
    quarter = size // 4
    terms = []
    for r in range(quarter):
        k = 4 * r + 1
        if k < size // 2:
            terms.append(found[k])
        else:
            value = found[size - k]
            terms.append((value[0], -value[1]))
    back = [turn(value, -n, size) for n, value in enumerate(dft(terms, -1))]
    return [v[0] for v in back] + [-v[1] for v in back]


def real_back(found, size):
    if size == 2:
        return [found[0][0] + found[1][0], found[0][0] - found[1][0]]
    half = size // 2
    even = real_back({k // 2: v for k, v in found.items() if k % 2 == 0}, half)
    odd = odd_back(found, size)
    return [even[n] + odd[n] for n in range(half)] + [even[n] - odd[n] for n in range(half)]


def padded_back(found, size):
    even = real_back({k // 2: v for k, v in found.items() if k % 2 == 0}, size)
    odd = odd_back(found, 2 * size)
    return [e + o for e, o in zip(even, odd)]


def long_tables(slabs, tokens):
    full = 2 * slabs * tokens
    token = np.arange(tokens)
    angle = 2.0 * np.pi * (np.arange(slabs + 1)[:, None] * token[None, :] % full) / full
    cos, sin = np.cos(angle), -np.sin(angle)
    back_scale = np.full((slabs + 1, 1), 2.0 / full)
    back_scale[0] = back_scale[slabs] = 1.0 / full
    inner = 2.0 * np.pi * (token[:, None] * token[None, :] % tokens) / tokens
    re, im = np.cos(inner), -np.sin(inner)
    forward = np.block([[re, im], [-im, re]])
    inverse = np.block([[re, -im], [im, re]])
    turns = [t.astype(np.float32) for t in (cos, sin, cos * back_scale, -sin * back_scale)]
    return turns, split_table(forward), split_table(inverse)


LANES = 128
SUBS = 16


def forward_slabs(source, turn_re, turn_im, parts):
    slabs, rows, tokens = source.shape
    lanes = min(tokens, LANES)
    subs = min(rows, SUBS)
    for lane in range(0, tokens, lanes):

        def tile(step, carry, lane=lane):
            at = pl.ds(pl.multiple_of(step * subs, subs), subs)
            values = [source[j, at, lane : lane + lanes].astype(F32) for j in range(slabs)]
            for k, (re, im) in padded_dft(values).items():
                cos = turn_re[k : k + 1, lane : lane + lanes]
                sin = turn_im[k : k + 1, lane : lane + lanes]
                if im is None:
                    out = (re * cos, re * sin)
                else:
                    out = (re * cos - im * sin, re * sin + im * cos)
                for part, value in enumerate(out):
                    where = slice(part * tokens + lane, part * tokens + lane + lanes)
                    store_split(parts, (k, at, where), value)
            return carry

        lax.fori_loop(0, rows // subs, tile, 0)


def store_split(parts, where, value):
    high = value.astype(BF16)
    parts[0][where] = high
    if len(parts) > 1:
        parts[1][where] = (value - high.astype(F32)).astype(BF16)


def product(parts, tables):
    slabs, rows, depth = parts[0].shape
    flat = [p[...].reshape(slabs * rows, depth) for p in parts]
    out = dot(flat[0], tables[0][...])
    for left, right in zip(flat[1:], tables):
        out += dot(left, right[...])
    for right in tables[1:]:
        out += dot(flat[0], right[...])
    return out.reshape(slabs, rows, depth)


def response_kernel(source, turn_re, turn_im, high, low, out, *parts):
    forward_slabs(source, turn_re, turn_im, parts)
    out[...] = product(parts, (high, low))


def multiply(spec, response, parts):
    tokens = spec.shape[2] // 2

    def one(k, carry):
        sig_re, sig_im = spec[k, :, :tokens], spec[k, :, tokens:]
        res_re, res_im = response[k, :, :tokens], response[k, :, tokens:]
        for part, value in enumerate(
            (sig_re * res_re - sig_im * res_im, sig_re * res_im + sig_im * res_re)
        ):
            where = (k, slice(None), slice(part * tokens, (part + 1) * tokens))
            store_split(parts, where, value)
        return carry

    lax.fori_loop(0, spec.shape[0], one, 0)


def back_slabs(spec, back_re, back_im, out):
    slabs, rows, tokens = out.shape
    lanes = min(tokens, LANES)
    subs = min(rows, SUBS)
    for lane in range(0, tokens, lanes):

        def tile(step, carry, lane=lane):
            at = pl.ds(pl.multiple_of(step * subs, subs), subs)
            found = {}
            for k in range(slabs + 1):
                re = spec[k, at, lane : lane + lanes]
                im = spec[k, at, tokens + lane : tokens + lane + lanes]
                cos = back_re[k : k + 1, lane : lane + lanes]
                sin = back_im[k : k + 1, lane : lane + lanes]
                if k in (0, slabs):
                    found[k] = (re * cos - im * sin, None)
                else:
                    found[k] = (re * cos - im * sin, re * sin + im * cos)
            for j, value in enumerate(padded_back(found, slabs)):
                out[j, at, lane : lane + lanes] = value.astype(BF16)
            return carry

        lax.fori_loop(0, rows // subs, tile, 0)


def convolve_kernel(
    block, source, response, turn_re, turn_im, back_re, back_im, forward, inverse, out, spec, part, held, sem
):
    convolve(block, source, response, (turn_re, turn_im, back_re, back_im), forward, inverse, out, spec, part, held, sem)


def convolve(block, source, response, turns, forward, inverse, out, spec, part, held, sem):
    rows = source.shape[1]
    turn_re, turn_im, back_re, back_im = turns
    copies = [
        pltpu.make_async_copy(
            response.at[:, pl.ds(i * block, block), :], held.at[i], sem.at[i]
        )
        for i in range(rows // block)
    ]
    for copy in copies:
        copy.start()
    for i, copy in enumerate(copies):
        at = pl.ds(i * block, block)
        forward_slabs(source.at[:, at, :], turn_re, turn_im, [part])
        spec[...] = product([part], (forward,))
        copy.wait()
        multiply(spec, held.at[i], [part])
        spec[...] = product([part], (inverse,))
        back_slabs(spec, back_re, back_im, out.at[:, at, :])


def pieces_kernel(pairs, block, chunk, where, *refs):
    own, (other, response, *turns, forward, inverse) = refs[:pairs], refs[pairs : pairs + 8]
    outs, (source, out, *scratch) = refs[pairs + 8 : 2 * pairs + 8], refs[2 * pairs + 8 :]
    chip, core = where[1], where[2]
    for rel in range(pairs):
        source[2 * (chip ^ rel) + core] = own[rel][0]
        source[2 * (chip ^ rel) + 1 - core] = other[rel]
    rows = source.shape[1]
    response = response.at[:, pl.ds(chunk * rows, rows), :]
    convolve(block, source, response, turns, forward, inverse, out, *scratch)
    for rel in range(pairs):
        for slot in range(2):
            outs[rel][slot] = out[2 * (chip ^ rel) + (core ^ slot)]


def convolve_call(where, source, response, tables, chunk=None, block=64):
    if chunk is None:
        slabs, rows, tokens = source.shape
    else:
        slabs, (_, rows, tokens) = 2 * len(source[0]), source[1].shape
    block = min(rows, block)
    turns, forward, inverse = tables
    here = pl.BlockSpec(memory_space=pltpu.VMEM)
    given = [*turns, forward[0], inverse[0]]
    specs = [pl.BlockSpec(memory_space=pl.ANY)] + [here] * len(given)
    wide = (slabs + 1, block, 2 * tokens)
    scratch = [
        pltpu.VMEM(wide, F32),
        pltpu.VMEM(wide, BF16),
        pltpu.VMEM((rows // block, *wide), F32),
        pltpu.SemaphoreType.DMA((rows // block,)),
    ]
    if chunk is None:
        body = functools.partial(convolve_kernel, block)
        args, specs = [source, response, *given], [here] + specs
        out_specs, out_shape = here, jax.ShapeDtypeStruct((slabs, rows, tokens), BF16)
    else:
        pairs = len(source[0])
        body = functools.partial(pieces_kernel, pairs, block, chunk)
        args = [where, *source[0], source[1], response, *given]
        specs = [pl.BlockSpec(memory_space=pltpu.SMEM)] + [here] * (pairs + 1) + specs
        out_specs = [here] * pairs
        out_shape = [jax.ShapeDtypeStruct((2, rows, tokens), BF16)] * pairs
        scratch = [pltpu.VMEM((slabs, rows, tokens), BF16)] * 2 + scratch
    return pl.pallas_call(
        body,
        in_specs=specs,
        out_specs=out_specs,
        out_shape=out_shape,
        scratch_shapes=scratch,
        compiler_params=pltpu.CompilerParams(vmem_limit_bytes=48 * MIB),
        cost_estimate=pl.CostEstimate(
            flops=16 * (slabs + 1) * rows * tokens * tokens, bytes_accessed=rows, transcendentals=0
        ),
    )(*args)


def response_call(source, tables, block=32):
    slabs, rows, tokens = source.shape
    block = min(rows, block)
    turns, forward, _ = tables
    given = [*turns[:2], *forward]
    wide = (slabs + 1, block, 2 * tokens)
    return pl.pallas_call(
        response_kernel,
        grid=(rows // block,),
        in_specs=[pl.BlockSpec((slabs, block, tokens), lambda i: (0, i, 0))]
        + [whole_spec(t) for t in given],
        out_specs=pl.BlockSpec(wide, lambda i: (0, i, 0)),
        out_shape=jax.ShapeDtypeStruct((slabs + 1, rows, 2 * tokens), F32),
        scratch_shapes=[pltpu.VMEM(wide, BF16)] * 2,
        compiler_params=pltpu.CompilerParams(vmem_limit_bytes=60 * MIB),
        cost_estimate=pl.CostEstimate(
            flops=24 * (slabs + 1) * rows * tokens * tokens, bytes_accessed=rows, transcendentals=0
        ),
    )(source, *given)


def gate_kernel(pairs, where, query, skip, given, *refs):
    pieces, (out, rows_out, sem) = refs[: CHUNKS * (pairs + 1)], refs[CHUNKS * (pairs + 1) :]
    chip, core = where[1], where[2]
    rows = pieces[0].shape[1]
    chip_rows = 2 * CHUNKS * rows
    copies = []
    for rel in range(pairs):
        for chunk in range(CHUNKS):
            own, other = pieces[chunk * (pairs + 1) + rel], pieces[chunk * (pairs + 1) + pairs]
            for slot, part in ((0, own[0]), (1, other[rel])):
                at = chunk_rows(chip ^ rel, core ^ slot, chunk, rows)
                direct = skip[at, :1] * given[at, :].astype(F32)
                result = query[at, :].astype(F32) * (part.astype(F32) + direct)
                rows_out[at, :] = result.astype(BF16)
        at = pl.ds(pl.multiple_of((chip ^ rel) * chip_rows, chip_rows), chip_rows)
        copies.append(pltpu.make_async_copy(rows_out.at[at, :], out.at[at, :], sem.at[rel]))
        copies[-1].start()
    for copy in copies:
        copy.wait()


def gate_call(where, query, skip, given, pieces, pairs):
    here = pl.BlockSpec(memory_space=pltpu.VMEM)
    flat = [p for own, other in pieces for p in (*own, other)]
    return pl.pallas_call(
        functools.partial(gate_kernel, pairs),
        in_specs=[pl.BlockSpec(memory_space=pltpu.SMEM)] + [here] * (3 + len(flat)),
        out_specs=pl.BlockSpec(memory_space=pl.ANY),
        out_shape=jax.ShapeDtypeStruct(query.shape, BF16),
        scratch_shapes=[pltpu.VMEM(query.shape, BF16), pltpu.SemaphoreType.DMA((pairs,))],
        compiler_params=pltpu.CompilerParams(vmem_limit_bytes=16 * MIB),
    )(where, query, skip, given, *flat)


def exchange(value, groups):
    rows, tokens = value.shape
    return lax.all_to_all(
        value.reshape(groups, rows // groups, tokens), "ctx", split_axis=0, concat_axis=0, tiled=True
    )


MOST_PAIRS = 0


def second_kernel(*refs):
    *pieces, out = refs
    for rel, piece in enumerate(pieces):
        out[rel] = piece[1]


def second_slots(pieces):
    here = pl.BlockSpec(memory_space=pltpu.VMEM)
    return pl.pallas_call(
        second_kernel,
        in_specs=[here] * len(pieces),
        out_specs=here,
        out_shape=jax.ShapeDtypeStruct((len(pieces), *pieces[0].shape[1:]), BF16),
        cost_estimate=pl.CostEstimate(
            flops=pieces[0].size, bytes_accessed=pieces[0].size, transcendentals=0
        ),
    )(*pieces)


def to_chips(pieces, groups):
    found = [pieces[0]]
    for rel in range(1, len(pieces)):
        found.append(lax.ppermute(pieces[rel], "ctx", [(i, i ^ (2 * rel)) for i in range(groups)]))
    second = second_slots(found)
    return found, lax.ppermute(second, "ctx", [(i, i ^ 1) for i in range(groups)])


def on_device(
    mr_query, mr_key, mr_value, mr_filter, proj_weight, li_query, li_key, li_filter, li_skip
):
    rows, tokens = mr_key.shape
    half = tokens // 2
    groups = lax.axis_size("ctx")
    pairs = groups // 2 if groups // 2 <= MOST_PAIRS else 0
    short = short_tables(tokens)
    tables = long_tables(groups, tokens)
    swap = [(0, 1), (1, 0)]
    mine = lax.axis_index("ch").astype(jnp.int32)
    slab = lax.axis_index("ctx").astype(jnp.int32)
    own = jnp.stack([mine, slab // 2, slab % 2])
    where = jnp.stack([1 - mine, slab // 2, slab % 2])

    late, border = short_conv(None, mr_key, mr_value, mr_query, mr_filter, short)
    border = lax.ppermute(border, "ctx", [(i, i + 1) for i in range(groups - 1)])
    other_late = lax.ppermute(late, "ch", swap)
    li_filter, late = lax.optimization_barrier((li_filter, late))
    filter_part = exchange(li_filter, groups)
    (early,) = short_conv(border, mr_key, mr_value, mr_query, mr_filter, short)
    other_early = lax.ppermute(early, "ch", swap)

    late_total, early_total = project_own(own, proj_weight, late, early)
    li_input, *pieces = project_other(
        where, proj_weight, other_late, other_early, late_total, early_total, li_key, pairs
    )
    response = response_call(filter_part, tables)
    if not pairs:
        long_part = convolve_call(where, exchange(li_input, groups), response, tables)
        long_local = exchange(long_part.reshape(rows, tokens), groups).reshape(rows, tokens)
        gated_out = li_query.astype(F32) * (
            long_local.astype(F32) + li_skip[:, None] * li_input.astype(F32)
        )
        return gated_out.astype(BF16)

    arrived = [to_chips(pieces[c * pairs : (c + 1) * pairs], groups) for c in range(CHUNKS)]
    returned = []
    for chunk, source in enumerate(arrived):
        back = convolve_call(where, source, response, tables, chunk)
        returned.append(to_chips(back, groups))
    skip = jnp.broadcast_to(li_skip[:, None], (rows, 128))
    return gate_call(where, li_query, skip, li_input, returned, pairs)


def solution(mesh):
    in_specs = (
        P("ch", "ctx"),
        P("ch", "ctx"),
        P("ch", "ctx"),
        P("ch", None),
        P("ch", None),
        P("ch", "ctx"),
        P("ch", "ctx"),
        P("ch", "ctx"),
        P("ch"),
    )
    return jax.shard_map(
        on_device, mesh=mesh, in_specs=in_specs, out_specs=P("ch", "ctx"), check_vma=False
    )
```

```python
import functools
import math

import jax
import jax.numpy as jnp
import numpy as np
from jax import lax
from jax.experimental import pallas as pl
from jax.experimental.pallas import tpu as pltpu
from jax.sharding import PartitionSpec as P

F32 = jnp.float32
BF16 = jnp.bfloat16
MIB = 1 << 20


def split_table(table):
    high = table.astype(np.float32).astype(BF16)
    low = (table - high.astype(np.float64)).astype(np.float32).astype(BF16)
    return np.asarray(high), np.asarray(low)


def split_value(value):
    high = value.astype(BF16)
    return high, (value - high.astype(F32)).astype(BF16)


def dot(left, right):
    return jnp.dot(left, right, preferred_element_type=F32)


def short_tables(size):
    half = size // 2
    time = np.arange(size)[:, None]
    freq = np.arange(half)[None, :]
    angle = 2.0 * np.pi * (time * freq % size) / size
    forward = np.concatenate([np.cos(angle), -np.sin(angle)], axis=1)
    forward[:, half] = np.where(np.arange(size) % 2 == 0, 1.0, -1.0)
    inverse = forward.T * (2.0 / size)
    inverse[0] /= 2.0
    inverse[half] /= 2.0
    return (*split_table(forward), np.concatenate(split_table(inverse[:, half:]), axis=1))


def short_filter(window, taps, query, fwd_hi, fwd_lo, inverse):
    half = taps.shape[1]
    spec = dot(window, fwd_hi) + dot(window, fwd_lo)
    taps_hi, taps_lo = split_value(taps)
    doubled = jnp.concatenate([fwd_hi[:half], fwd_hi[:half]], axis=0)
    resp = dot(jnp.concatenate([taps_hi, taps_lo], axis=1), doubled) + dot(taps_hi, fwd_lo[:half])
    first = lax.broadcasted_iota(jnp.int32, (taps.shape[0], half), 1) == 0
    resp_re, resp_im = resp[:, :half], resp[:, half:]
    cross = jnp.where(first, 0.0, resp_im)
    own = jnp.where(first, resp_im, resp_re)
    spec_re, spec_im = spec[:, :half], spec[:, half:]
    prod = jnp.concatenate(
        [spec_re * resp_re - spec_im * cross, spec_re * cross + spec_im * own], axis=1
    )
    prod_hi, prod_lo = split_value(prod)
    both = dot(prod_hi, inverse)
    mixed = both[:, :half] + both[:, half:] + dot(prod_lo, inverse[:, :half])
    return (query.astype(F32) * mixed).astype(BF16)


def gate_input(key, value):
    return (key.astype(F32) * value.astype(F32)).astype(BF16)


def late_kernel(key, value, query, taps, fwd_hi, fwd_lo, inverse, out, border):
    window = gate_input(key[...], value[...])
    border[...] = window[:, query.shape[1] :]
    out[...] = short_filter(
        window, taps[...], query[...], fwd_hi[...], fwd_lo[...], inverse[...]
    )


def early_kernel(border, key, value, query, taps, fwd_hi, fwd_lo, inverse, out):
    window = jnp.concatenate([border[...], gate_input(key[...], value[...])], axis=1)
    out[...] = short_filter(
        window, taps[...], query[...], fwd_hi[...], fwd_lo[...], inverse[...]
    )


def whole_spec(array):
    return pl.BlockSpec(array.shape, lambda *_: (0,) * array.ndim)


def short_conv(border, key, value, query, taps, tables, block=1024):
    rows, tokens = key.shape
    half = tokens // 2
    block = min(rows, block)
    table_specs = [whole_spec(t) for t in tables]
    full = pl.BlockSpec((block, tokens), lambda i: (i, 0))
    left = pl.BlockSpec((block, half), lambda i: (i, 0))
    right = pl.BlockSpec((block, half), lambda i: (i, 1))
    if border is None:
        body, specs, outs = late_kernel, [full, full, right, left], 2
        args = (key, value, query, taps)
    else:
        body, specs, outs = early_kernel, [left, left, left, left, left], 1
        args = (border, key, value, query, taps)
    return pl.pallas_call(
        body,
        grid=(rows // block,),
        in_specs=specs + table_specs,
        out_specs=[left] * outs,
        out_shape=[jax.ShapeDtypeStruct((rows, half), BF16)] * outs,
        compiler_params=pltpu.CompilerParams(vmem_limit_bytes=(60 if border is None else 48) * MIB),
        cost_estimate=pl.CostEstimate(
            flops=50 * rows * tokens * tokens, bytes_accessed=8 * rows * tokens, transcendentals=0
        ),
    )(*args, *tables)


def own_kernel(which, weight, late, early, late_out, early_out):
    del which
    half = late.shape[1]
    found = dot(weight[...], jnp.concatenate([late[...], early[...]], axis=1))
    late_out[...] = found[:, :half]
    early_out[...] = found[:, half:]


def other_kernel(which, weight, piece, total, key, *refs):
    del which
    values = total[...] + dot(weight[...], piece[...])
    refs[-1][...] = (key[...].astype(F32) * values).astype(BF16)


BLOCK = 1024


def project_own(which, weight, late, early):
    rows, (depth, half) = weight.shape[0], late.shape
    block = min(rows, BLOCK)
    whole = pl.BlockSpec((depth, half), lambda i, w: (0, 0))
    moving = pl.BlockSpec((block, half), lambda i, w: (i, 0))
    return pl.pallas_call(
        own_kernel,
        grid_spec=pltpu.PrefetchScalarGridSpec(
            num_scalar_prefetch=1,
            grid=(rows // block,),
            in_specs=[pl.BlockSpec((block, depth), lambda i, w: (i, w[0])), whole, whole],
            out_specs=[moving, moving],
        ),
        out_shape=[jax.ShapeDtypeStruct((rows, half), F32)] * 2,
        compiler_params=pltpu.CompilerParams(vmem_limit_bytes=VMEM_PROJECT),
        cost_estimate=pl.CostEstimate(
            flops=4 * rows * depth * half, bytes_accessed=2 * rows * depth, transcendentals=0
        ),
    )(which, weight, late, early)


VMEM_PROJECT = 46 * MIB


def project_other(which, weight, piece, total, key, side, given=None):
    rows, (depth, half) = weight.shape[0], piece.shape
    block = min(rows, BLOCK)
    at_side = pl.BlockSpec((block, half), lambda i, w: (i, side))
    specs = [
        pl.BlockSpec((block, depth), lambda i, w: (i, w[0])),
        pl.BlockSpec((depth, half), lambda i, w: (0, 0)),
        pl.BlockSpec((block, half), lambda i, w: (i, 0)),
        at_side,
    ]
    args = [weight, piece, total, key]
    if given is not None:
        specs.append(pl.BlockSpec(memory_space=pl.ANY))
        args.append(given)
    return pl.pallas_call(
        other_kernel,
        grid_spec=pltpu.PrefetchScalarGridSpec(
            num_scalar_prefetch=1, grid=(rows // block,), in_specs=specs, out_specs=at_side
        ),
        out_shape=jax.ShapeDtypeStruct((rows, 2 * half), BF16),
        input_output_aliases={} if given is None else {5: 0},
        compiler_params=pltpu.CompilerParams(vmem_limit_bytes=VMEM_PROJECT),
        cost_estimate=pl.CostEstimate(
            flops=16 * rows * depth * half, bytes_accessed=2 * rows * depth, transcendentals=0
        ),
    )(which, *args)


def turn(value, num, den):
    num %= den
    if num < 0:
        num += den
    re, im = value
    if num == 0:
        return value
    if 4 * num == den:
        return (im, -re)
    if 2 * num == den:
        return (-re, -im)
    if 4 * num == 3 * den:
        return (-im, re)
    cos = math.cos(2.0 * math.pi * num / den)
    sin = math.sin(2.0 * math.pi * num / den)
    if 8 * num % den == 0:
        size = math.sqrt(0.5)
        cos, sin = (1 if cos > 0 else -1), (1 if sin > 0 else -1)
        first = re + im if cos == sin else re - im
        second = im - re if cos == sin else im + re
        if cos > 0:
            return (size * first, size * second)
        return ((-size) * first, (-size) * second)
    return (cos * re + sin * im, cos * im - sin * re)


def add(a, b):
    return (a[0] + b[0], a[1] + b[1])


def sub(a, b):
    return (a[0] - b[0], a[1] - b[1])


def dft(values, sign):
    size = len(values)
    if size == 1:
        return values
    half = size // 2
    even = dft([add(values[n], values[n + half]) for n in range(half)], sign)
    odd = dft(
        [turn(sub(values[n], values[n + half]), sign * n, size) for n in range(half)], sign
    )
    out = []
    for n in range(half):
        out += [even[n], odd[n]]
    return out


def odd_part(values, size):
    half = len(values) // 2
    shaped = [turn((values[n], -values[n + half]), n, size) for n in range(half)]
    found = {}
    for r, value in enumerate(dft(shaped, 1)):
        k = 4 * r + 1
        if k < size // 2:
            found[k] = value
        else:
            found[size - k] = (value[0], -value[1])
    return found


def real_dft(values):
    size = len(values)
    if size == 2:
        return {0: (values[0] + values[1], None), 1: (values[0] - values[1], None)}
    half = size // 2
    found = {
        2 * k: v
        for k, v in real_dft([values[n] + values[n + half] for n in range(half)]).items()
    }
    found.update(odd_part([values[n] - values[n + half] for n in range(half)], size))
    return found


def padded_dft(values):
    found = {2 * k: v for k, v in real_dft(values).items()}
    found.update(odd_part(values, 2 * len(values)))
    return found


def odd_back(found, size):
    quarter = size // 4
    terms = []
    for r in range(quarter):
        k = 4 * r + 1
        if k < size // 2:
            terms.append(found[k])
        else:
            value = found[size - k]
            terms.append((value[0], -value[1]))
    back = [turn(value, -n, size) for n, value in enumerate(dft(terms, -1))]
    return [v[0] for v in back] + [-v[1] for v in back]


def real_back(found, size):
    if size == 2:
        return [found[0][0] + found[1][0], found[0][0] - found[1][0]]
    half = size // 2
    even = real_back({k // 2: v for k, v in found.items() if k % 2 == 0}, half)
    odd = odd_back(found, size)
    return [even[n] + odd[n] for n in range(half)] + [even[n] - odd[n] for n in range(half)]


def padded_back(found, size):
    even = real_back({k // 2: v for k, v in found.items() if k % 2 == 0}, size)
    odd = odd_back(found, 2 * size)
    return [e + o for e, o in zip(even, odd)]


def long_tables(slabs, tokens):
    full = 2 * slabs * tokens
    token = np.arange(tokens)
    angle = 2.0 * np.pi * (np.arange(slabs + 1)[:, None] * token[None, :] % full) / full
    cos, sin = np.cos(angle), -np.sin(angle)
    back_scale = np.full((slabs + 1, 1), 2.0 / full)
    back_scale[0] = back_scale[slabs] = 1.0 / full
    inner = 2.0 * np.pi * (token[:, None] * token[None, :] % tokens) / tokens
    re, im = np.cos(inner), -np.sin(inner)
    forward = np.block([[re, im], [-im, re]])
    inverse = np.block([[re, -im], [im, re]])
    turns = [t.astype(np.float32) for t in (cos, sin, cos * back_scale, -sin * back_scale)]
    return turns, split_table(forward), split_table(inverse)


LANES = 128
SUBS = 16


def forward_slabs(source, turn_re, turn_im, parts):
    slabs, rows, tokens = source.shape
    lanes = min(tokens, LANES)
    subs = min(rows, SUBS)
    for lane in range(0, tokens, lanes):

        def tile(step, carry, lane=lane):
            at = pl.ds(pl.multiple_of(step * subs, subs), subs)
            values = [source[j, at, lane : lane + lanes].astype(F32) for j in range(slabs)]
            for k, (re, im) in padded_dft(values).items():
                cos = turn_re[k : k + 1, lane : lane + lanes]
                sin = turn_im[k : k + 1, lane : lane + lanes]
                if im is None:
                    out = (re * cos, re * sin)
                else:
                    out = (re * cos - im * sin, re * sin + im * cos)
                for part, value in enumerate(out):
                    where = slice(part * tokens + lane, part * tokens + lane + lanes)
                    store_split(parts, (k, at, where), value)
            return carry

        lax.fori_loop(0, rows // subs, tile, 0)


def store_split(parts, where, value):
    high = value.astype(BF16)
    parts[0][where] = high
    if len(parts) > 1:
        parts[1][where] = (value - high.astype(F32)).astype(BF16)


def product(parts, tables):
    slabs, rows, depth = parts[0].shape
    flat = [p[...].reshape(slabs * rows, depth) for p in parts]
    out = dot(flat[0], tables[0][...])
    for left, right in zip(flat[1:], tables):
        out += dot(left, right[...])
    for right in tables[1:]:
        out += dot(flat[0], right[...])
    return out.reshape(slabs, rows, depth)


def response_kernel(source, turn_re, turn_im, high, low, out, *parts):
    forward_slabs(source, turn_re, turn_im, parts)
    out[...] = product(parts, (high, low))


def multiply(spec, response, parts):
    tokens = spec.shape[2] // 2

    def one(k, carry):
        sig_re, sig_im = spec[k, :, :tokens], spec[k, :, tokens:]
        res_re, res_im = response[k, :, :tokens], response[k, :, tokens:]
        for part, value in enumerate(
            (sig_re * res_re - sig_im * res_im, sig_re * res_im + sig_im * res_re)
        ):
            where = (k, slice(None), slice(part * tokens, (part + 1) * tokens))
            store_split(parts, where, value)
        return carry

    lax.fori_loop(0, spec.shape[0], one, 0)


def back_slabs(spec, back_re, back_im, out):
    slabs, rows, tokens = out.shape
    lanes = min(tokens, LANES)
    subs = min(rows, SUBS)
    for lane in range(0, tokens, lanes):

        def tile(step, carry, lane=lane):
            at = pl.ds(pl.multiple_of(step * subs, subs), subs)
            found = {}
            for k in range(slabs + 1):
                re = spec[k, at, lane : lane + lanes]
                im = spec[k, at, tokens + lane : tokens + lane + lanes]
                cos = back_re[k : k + 1, lane : lane + lanes]
                sin = back_im[k : k + 1, lane : lane + lanes]
                if k in (0, slabs):
                    found[k] = (re * cos - im * sin, None)
                else:
                    found[k] = (re * cos - im * sin, re * sin + im * cos)
            for j, value in enumerate(padded_back(found, slabs)):
                out[j, at, lane : lane + lanes] = value.astype(BF16)
            return carry

        lax.fori_loop(0, rows // subs, tile, 0)


def convolve_kernel(
    block, source, response, turn_re, turn_im, back_re, back_im, forward, inverse, out, spec, part, held, sem
):
    copies = []
    for i in range(source.shape[1] // block):
        rows = pl.ds(i * block, block)
        copies.append(pltpu.make_async_copy(response.at[:, rows, :], held.at[i], sem.at[i]))
        copies[-1].start()
    for i, copy in enumerate(copies):
        rows = pl.ds(i * block, block)
        forward_slabs(source.at[:, rows, :], turn_re, turn_im, [part])
        spec[...] = product([part], (forward,))
        copy.wait()
        multiply(spec, held.at[i], [part])
        spec[...] = product([part], (inverse,))
        back_slabs(spec, back_re, back_im, out.at[:, rows, :])


def convolve_call(source, response, tables, block=64):
    slabs, rows, tokens = source.shape
    block = min(rows, block)
    turns, forward, inverse = tables
    here = pl.BlockSpec(memory_space=pltpu.VMEM)
    wide = (slabs + 1, block, 2 * tokens)
    return pl.pallas_call(
        functools.partial(convolve_kernel, block),
        in_specs=[here, pl.BlockSpec(memory_space=pl.ANY)] + [here] * 6,
        out_specs=here,
        out_shape=jax.ShapeDtypeStruct((slabs, rows, tokens), BF16),
        scratch_shapes=[
            pltpu.VMEM(wide, F32),
            pltpu.VMEM(wide, BF16),
            pltpu.VMEM((rows // block, *wide), F32),
            pltpu.SemaphoreType.DMA((rows // block,)),
        ],
        compiler_params=pltpu.CompilerParams(vmem_limit_bytes=48 * MIB),
        cost_estimate=pl.CostEstimate(
            flops=16 * (slabs + 1) * rows * tokens * tokens, bytes_accessed=rows, transcendentals=0
        ),
    )(source, response, *turns, forward[0], inverse[0])


def response_call(source, tables, block=32):
    slabs, rows, tokens = source.shape
    block = min(rows, block)
    turns, forward, _ = tables
    given = [*turns[:2], *forward]
    wide = (slabs + 1, block, 2 * tokens)
    return pl.pallas_call(
        response_kernel,
        grid=(rows // block,),
        in_specs=[pl.BlockSpec((slabs, block, tokens), lambda i: (0, i, 0))]
        + [whole_spec(t) for t in given],
        out_specs=pl.BlockSpec(wide, lambda i: (0, i, 0)),
        out_shape=jax.ShapeDtypeStruct((slabs + 1, rows, 2 * tokens), F32),
        scratch_shapes=[pltpu.VMEM(wide, BF16)] * 2,
        compiler_params=pltpu.CompilerParams(vmem_limit_bytes=60 * MIB),
        cost_estimate=pl.CostEstimate(
            flops=24 * (slabs + 1) * rows * tokens * tokens, bytes_accessed=rows, transcendentals=0
        ),
    )(source, *given)


def exchange(value, groups):
    rows, tokens = value.shape
    return lax.all_to_all(
        value.reshape(groups, rows // groups, tokens), "ctx", split_axis=0, concat_axis=0, tiled=True
    )


def on_device(
    mr_query, mr_key, mr_value, mr_filter, proj_weight, li_query, li_key, li_filter, li_skip
):
    rows, tokens = mr_key.shape
    half = tokens // 2
    groups = lax.axis_size("ctx")
    short = short_tables(tokens)
    tables = long_tables(groups, tokens)
    swap = [(0, 1), (1, 0)]
    mine = lax.axis_index("ch").astype(jnp.int32).reshape(1)

    late, border = short_conv(None, mr_key, mr_value, mr_query, mr_filter, short)
    border = lax.ppermute(border, "ctx", [(i, i + 1) for i in range(groups - 1)])
    other_late = lax.ppermute(late, "ch", swap)
    li_filter, late = lax.optimization_barrier((li_filter, late))
    filter_part = exchange(li_filter, groups)
    (early,) = short_conv(border, mr_key, mr_value, mr_query, mr_filter, short)
    other_early = lax.ppermute(early, "ch", swap)

    late_total, early_total = project_own(mine, proj_weight, late, early)
    li_input = project_other(1 - mine, proj_weight, other_late, late_total, li_key, 1)
    li_input = project_other(1 - mine, proj_weight, other_early, early_total, li_key, 0, li_input)

    direct = li_skip[:, None] * li_input.astype(F32)
    response, direct = lax.optimization_barrier((response_call(filter_part, tables), direct))
    long_part = convolve_call(exchange(li_input, groups), response, tables)
    long_local = exchange(long_part.reshape(rows, tokens), groups).reshape(rows, tokens)
    gated_out = li_query.astype(F32) * (long_local.astype(F32) + direct)
    return gated_out.astype(BF16)


def solution(mesh):
    in_specs = (
        P("ch", "ctx"),
        P("ch", "ctx"),
        P("ch", "ctx"),
        P("ch", None),
        P("ch", None),
        P("ch", "ctx"),
        P("ch", "ctx"),
        P("ch", "ctx"),
        P("ch"),
    )
    return jax.shard_map(
        on_device, mesh=mesh, in_specs=in_specs, out_specs=P("ch", "ctx"), check_vma=False
    )
```

```python
import functools
import math

import jax
import jax.numpy as jnp
import numpy as np
from jax import lax
from jax.experimental import pallas as pl
from jax.experimental.pallas import tpu as pltpu
from jax.sharding import PartitionSpec as P

F32 = jnp.float32
BF16 = jnp.bfloat16
MIB = 1 << 20


def split_table(table):
    high = table.astype(np.float32).astype(BF16)
    low = (table - high.astype(np.float64)).astype(np.float32).astype(BF16)
    return np.asarray(high), np.asarray(low)


def split_value(value):
    high = value.astype(BF16)
    return high, (value - high.astype(F32)).astype(BF16)


def dot(left, right):
    return jnp.dot(left, right, preferred_element_type=F32)


def short_tables(size):
    half = size // 2
    time = np.arange(size)[:, None]
    freq = np.arange(half)[None, :]
    angle = 2.0 * np.pi * (time * freq % size) / size
    forward = np.concatenate([np.cos(angle), -np.sin(angle)], axis=1)
    forward[:, half] = np.where(np.arange(size) % 2 == 0, 1.0, -1.0)
    inverse = forward.T * (2.0 / size)
    inverse[0] /= 2.0
    inverse[half] /= 2.0
    return (*split_table(forward), np.concatenate(split_table(inverse[:, half:]), axis=1))


def short_filter(window, taps, query, fwd_hi, fwd_lo, inverse):
    half = taps.shape[1]
    spec = dot(window, fwd_hi) + dot(window, fwd_lo)
    taps_hi, taps_lo = split_value(taps)
    doubled = jnp.concatenate([fwd_hi[:half], fwd_hi[:half]], axis=0)
    resp = dot(jnp.concatenate([taps_hi, taps_lo], axis=1), doubled) + dot(taps_hi, fwd_lo[:half])
    first = lax.broadcasted_iota(jnp.int32, (taps.shape[0], half), 1) == 0
    resp_re, resp_im = resp[:, :half], resp[:, half:]
    cross = jnp.where(first, 0.0, resp_im)
    own = jnp.where(first, resp_im, resp_re)
    spec_re, spec_im = spec[:, :half], spec[:, half:]
    prod = jnp.concatenate(
        [spec_re * resp_re - spec_im * cross, spec_re * cross + spec_im * own], axis=1
    )
    prod_hi, prod_lo = split_value(prod)
    both = dot(prod_hi, inverse)
    mixed = both[:, :half] + both[:, half:] + dot(prod_lo, inverse[:, :half])
    return (query.astype(F32) * mixed).astype(BF16)


def gate_input(key, value):
    return (key.astype(F32) * value.astype(F32)).astype(BF16)


def late_kernel(key, value, query, taps, fwd_hi, fwd_lo, inverse, out, border):
    window = gate_input(key[...], value[...])
    border[...] = window[:, query.shape[1] :]
    out[...] = short_filter(
        window, taps[...], query[...], fwd_hi[...], fwd_lo[...], inverse[...]
    )


def early_kernel(border, key, value, query, taps, fwd_hi, fwd_lo, inverse, out):
    window = jnp.concatenate([border[...], gate_input(key[...], value[...])], axis=1)
    out[...] = short_filter(
        window, taps[...], query[...], fwd_hi[...], fwd_lo[...], inverse[...]
    )


def whole_spec(array):
    return pl.BlockSpec(array.shape, lambda *_: (0,) * array.ndim)


def short_conv(border, key, value, query, taps, tables, block=1024):
    rows, tokens = key.shape
    half = tokens // 2
    block = min(rows, block)
    table_specs = [whole_spec(t) for t in tables]
    full = pl.BlockSpec((block, tokens), lambda i: (i, 0))
    left = pl.BlockSpec((block, half), lambda i: (i, 0))
    right = pl.BlockSpec((block, half), lambda i: (i, 1))
    if border is None:
        body, specs, outs = late_kernel, [full, full, right, left], 2
        args = (key, value, query, taps)
    else:
        body, specs, outs = early_kernel, [left, left, left, left, left], 1
        args = (border, key, value, query, taps)
    return pl.pallas_call(
        body,
        grid=(rows // block,),
        in_specs=specs + table_specs,
        out_specs=[left] * outs,
        out_shape=[jax.ShapeDtypeStruct((rows, half), BF16)] * outs,
        compiler_params=pltpu.CompilerParams(vmem_limit_bytes=(60 if border is None else 48) * MIB),
        cost_estimate=pl.CostEstimate(
            flops=50 * rows * tokens * tokens, bytes_accessed=8 * rows * tokens, transcendentals=0
        ),
    )(*args, *tables)


def own_kernel(which, weight, late, early, late_out, early_out):
    del which
    half = late.shape[1]
    found = dot(weight[...], jnp.concatenate([late[...], early[...]], axis=1))
    late_out[...] = found[:, :half]
    early_out[...] = found[:, half:]


def other_kernel(which, weight, piece, total, key, *refs):
    del which
    values = total[...] + dot(weight[...], piece[...])
    refs[-1][...] = (key[...].astype(F32) * values).astype(BF16)


BLOCK = 1024


def project_own(which, weight, late, early):
    rows, (depth, half) = weight.shape[0], late.shape
    block = min(rows, BLOCK)
    whole = pl.BlockSpec((depth, half), lambda i, w: (0, 0))
    moving = pl.BlockSpec((block, half), lambda i, w: (i, 0))
    return pl.pallas_call(
        own_kernel,
        grid_spec=pltpu.PrefetchScalarGridSpec(
            num_scalar_prefetch=1,
            grid=(rows // block,),
            in_specs=[pl.BlockSpec((block, depth), lambda i, w: (i, w[0])), whole, whole],
            out_specs=[moving, moving],
        ),
        out_shape=[jax.ShapeDtypeStruct((rows, half), F32)] * 2,
        compiler_params=pltpu.CompilerParams(vmem_limit_bytes=VMEM_PROJECT),
        cost_estimate=pl.CostEstimate(
            flops=4 * rows * depth * half, bytes_accessed=2 * rows * depth, transcendentals=0
        ),
    )(which, weight, late, early)


VMEM_PROJECT = 46 * MIB


def project_other(which, weight, piece, total, key, side, given=None):
    rows, (depth, half) = weight.shape[0], piece.shape
    block = min(rows, BLOCK)
    at_side = pl.BlockSpec((block, half), lambda i, w: (i, side))
    specs = [
        pl.BlockSpec((block, depth), lambda i, w: (i, w[0])),
        pl.BlockSpec((depth, half), lambda i, w: (0, 0)),
        pl.BlockSpec((block, half), lambda i, w: (i, 0)),
        at_side,
    ]
    args = [weight, piece, total, key]
    if given is not None:
        specs.append(pl.BlockSpec(memory_space=pl.ANY))
        args.append(given)
    return pl.pallas_call(
        other_kernel,
        grid_spec=pltpu.PrefetchScalarGridSpec(
            num_scalar_prefetch=1, grid=(rows // block,), in_specs=specs, out_specs=at_side
        ),
        out_shape=jax.ShapeDtypeStruct((rows, 2 * half), BF16),
        input_output_aliases={} if given is None else {5: 0},
        compiler_params=pltpu.CompilerParams(vmem_limit_bytes=VMEM_PROJECT),
        cost_estimate=pl.CostEstimate(
            flops=16 * rows * depth * half, bytes_accessed=2 * rows * depth, transcendentals=0
        ),
    )(which, *args)


def turn(value, num, den):
    num %= den
    if num < 0:
        num += den
    re, im = value
    if num == 0:
        return value
    if 4 * num == den:
        return (im, -re)
    if 2 * num == den:
        return (-re, -im)
    if 4 * num == 3 * den:
        return (-im, re)
    cos = math.cos(2.0 * math.pi * num / den)
    sin = math.sin(2.0 * math.pi * num / den)
    if 8 * num % den == 0:
        size = math.sqrt(0.5)
        cos, sin = (1 if cos > 0 else -1), (1 if sin > 0 else -1)
        first = re + im if cos == sin else re - im
        second = im - re if cos == sin else im + re
        if cos > 0:
            return (size * first, size * second)
        return ((-size) * first, (-size) * second)
    return (cos * re + sin * im, cos * im - sin * re)


def add(a, b):
    return (a[0] + b[0], a[1] + b[1])


def sub(a, b):
    return (a[0] - b[0], a[1] - b[1])


def dft(values, sign):
    size = len(values)
    if size == 1:
        return values
    half = size // 2
    even = dft([add(values[n], values[n + half]) for n in range(half)], sign)
    odd = dft(
        [turn(sub(values[n], values[n + half]), sign * n, size) for n in range(half)], sign
    )
    out = []
    for n in range(half):
        out += [even[n], odd[n]]
    return out


def odd_part(values, size):
    half = len(values) // 2
    shaped = [turn((values[n], -values[n + half]), n, size) for n in range(half)]
    found = {}
    for r, value in enumerate(dft(shaped, 1)):
        k = 4 * r + 1
        if k < size // 2:
            found[k] = value
        else:
            found[size - k] = (value[0], -value[1])
    return found


def real_dft(values):
    size = len(values)
    if size == 2:
        return {0: (values[0] + values[1], None), 1: (values[0] - values[1], None)}
    half = size // 2
    found = {
        2 * k: v
        for k, v in real_dft([values[n] + values[n + half] for n in range(half)]).items()
    }
    found.update(odd_part([values[n] - values[n + half] for n in range(half)], size))
    return found


def padded_dft(values):
    found = {2 * k: v for k, v in real_dft(values).items()}
    found.update(odd_part(values, 2 * len(values)))
    return found


def odd_back(found, size):
    quarter = size // 4
    terms = []
    for r in range(quarter):
        k = 4 * r + 1
        if k < size // 2:
            terms.append(found[k])
        else:
            value = found[size - k]
            terms.append((value[0], -value[1]))
    back = [turn(value, -n, size) for n, value in enumerate(dft(terms, -1))]
    return [v[0] for v in back] + [-v[1] for v in back]


def real_back(found, size):
    if size == 2:
        return [found[0][0] + found[1][0], found[0][0] - found[1][0]]
    half = size // 2
    even = real_back({k // 2: v for k, v in found.items() if k % 2 == 0}, half)
    odd = odd_back(found, size)
    return [even[n] + odd[n] for n in range(half)] + [even[n] - odd[n] for n in range(half)]


def padded_back(found, size):
    even = real_back({k // 2: v for k, v in found.items() if k % 2 == 0}, size)
    odd = odd_back(found, 2 * size)
    return [e + o for e, o in zip(even, odd)]


def long_tables(slabs, tokens):
    full = 2 * slabs * tokens
    token = np.arange(tokens)
    angle = 2.0 * np.pi * (np.arange(slabs + 1)[:, None] * token[None, :] % full) / full
    cos, sin = np.cos(angle), -np.sin(angle)
    back_scale = np.full((slabs + 1, 1), 2.0 / full)
    back_scale[0] = back_scale[slabs] = 1.0 / full
    inner = 2.0 * np.pi * (token[:, None] * token[None, :] % tokens) / tokens
    re, im = np.cos(inner), -np.sin(inner)
    forward = np.block([[re, im], [-im, re]])
    inverse = np.block([[re, -im], [im, re]])
    turns = [t.astype(np.float32) for t in (cos, sin, cos * back_scale, -sin * back_scale)]
    return turns, split_table(forward), split_table(inverse)


LANES = 128
SUBS = 32


def forward_slabs(source, turn_re, turn_im, parts):
    slabs, rows, tokens = source.shape
    lanes = min(tokens, LANES)
    subs = min(rows, SUBS)
    for lane in range(0, tokens, lanes):

        def tile(step, carry, lane=lane):
            at = pl.ds(pl.multiple_of(step * subs, subs), subs)
            values = [source[j, at, lane : lane + lanes].astype(F32) for j in range(slabs)]
            for k, (re, im) in padded_dft(values).items():
                cos = turn_re[k : k + 1, lane : lane + lanes]
                sin = turn_im[k : k + 1, lane : lane + lanes]
                if im is None:
                    out = (re * cos, re * sin)
                else:
                    out = (re * cos - im * sin, re * sin + im * cos)
                for part, value in enumerate(out):
                    where = slice(part * tokens + lane, part * tokens + lane + lanes)
                    store_split(parts, (k, at, where), value)
            return carry

        lax.fori_loop(0, rows // subs, tile, 0)


def store_split(parts, where, value):
    high = value.astype(BF16)
    parts[0][where] = high
    if len(parts) > 1:
        parts[1][where] = (value - high.astype(F32)).astype(BF16)


def product(parts, tables):
    slabs, rows, depth = parts[0].shape
    flat = [p[...].reshape(slabs * rows, depth) for p in parts]
    out = dot(flat[0], tables[0][...])
    for left, right in zip(flat[1:], tables):
        out += dot(left, right[...])
    for right in tables[1:]:
        out += dot(flat[0], right[...])
    return out.reshape(slabs, rows, depth)


def response_kernel(source, turn_re, turn_im, high, low, out, *parts):
    forward_slabs(source, turn_re, turn_im, parts)
    out[...] = product(parts, (high, low))


def multiply(spec, response, parts):
    tokens = spec.shape[2] // 2

    def one(k, carry):
        sig_re, sig_im = spec[k, :, :tokens], spec[k, :, tokens:]
        res_re, res_im = response[k, :, :tokens], response[k, :, tokens:]
        for part, value in enumerate(
            (sig_re * res_re - sig_im * res_im, sig_re * res_im + sig_im * res_re)
        ):
            where = (k, slice(None), slice(part * tokens, (part + 1) * tokens))
            store_split(parts, where, value)
        return carry

    lax.fori_loop(0, spec.shape[0], one, 0)


def back_slabs(spec, back_re, back_im, out):
    slabs, rows, tokens = out.shape
    lanes = min(tokens, LANES)
    subs = min(rows, SUBS)
    for lane in range(0, tokens, lanes):

        def tile(step, carry, lane=lane):
            at = pl.ds(pl.multiple_of(step * subs, subs), subs)
            found = {}
            for k in range(slabs + 1):
                re = spec[k, at, lane : lane + lanes]
                im = spec[k, at, tokens + lane : tokens + lane + lanes]
                cos = back_re[k : k + 1, lane : lane + lanes]
                sin = back_im[k : k + 1, lane : lane + lanes]
                if k in (0, slabs):
                    found[k] = (re * cos - im * sin, None)
                else:
                    found[k] = (re * cos - im * sin, re * sin + im * cos)
            for j, value in enumerate(padded_back(found, slabs)):
                out[j, at, lane : lane + lanes] = value.astype(BF16)
            return carry

        lax.fori_loop(0, rows // subs, tile, 0)


def convolve_kernel(
    block, source, response, turn_re, turn_im, back_re, back_im, forward, inverse, out, spec, part, held, sem
):
    copies = []
    for i in range(source.shape[1] // block):
        rows = pl.ds(i * block, block)
        copies.append(pltpu.make_async_copy(response.at[:, rows, :], held.at[i], sem.at[i]))
        copies[-1].start()
    for i, copy in enumerate(copies):
        rows = pl.ds(i * block, block)
        forward_slabs(source.at[:, rows, :], turn_re, turn_im, [part])
        spec[...] = product([part], (forward,))
        copy.wait()
        multiply(spec, held.at[i], [part])
        spec[...] = product([part], (inverse,))
        back_slabs(spec, back_re, back_im, out.at[:, rows, :])


def convolve_call(source, response, tables, block=128):
    slabs, rows, tokens = source.shape
    block = min(rows, block)
    turns, forward, inverse = tables
    here = pl.BlockSpec(memory_space=pltpu.VMEM)
    wide = (slabs + 1, block, 2 * tokens)
    return pl.pallas_call(
        functools.partial(convolve_kernel, block),
        in_specs=[here, pl.BlockSpec(memory_space=pl.ANY)] + [here] * 6,
        out_specs=here,
        out_shape=jax.ShapeDtypeStruct((slabs, rows, tokens), BF16),
        scratch_shapes=[
            pltpu.VMEM(wide, F32),
            pltpu.VMEM(wide, BF16),
            pltpu.VMEM((rows // block, *wide), F32),
            pltpu.SemaphoreType.DMA((rows // block,)),
        ],
        compiler_params=pltpu.CompilerParams(vmem_limit_bytes=48 * MIB),
        cost_estimate=pl.CostEstimate(
            flops=16 * (slabs + 1) * rows * tokens * tokens, bytes_accessed=rows, transcendentals=0
        ),
    )(source, response, *turns, forward[0], inverse[0])


def response_call(source, tables, block=32):
    slabs, rows, tokens = source.shape
    block = min(rows, block)
    turns, forward, _ = tables
    given = [*turns[:2], *forward]
    wide = (slabs + 1, block, 2 * tokens)
    return pl.pallas_call(
        response_kernel,
        grid=(rows // block,),
        in_specs=[pl.BlockSpec((slabs, block, tokens), lambda i: (0, i, 0))]
        + [whole_spec(t) for t in given],
        out_specs=pl.BlockSpec(wide, lambda i: (0, i, 0)),
        out_shape=jax.ShapeDtypeStruct((slabs + 1, rows, 2 * tokens), F32),
        scratch_shapes=[pltpu.VMEM(wide, BF16)] * 2,
        compiler_params=pltpu.CompilerParams(vmem_limit_bytes=60 * MIB),
        cost_estimate=pl.CostEstimate(
            flops=24 * (slabs + 1) * rows * tokens * tokens, bytes_accessed=rows, transcendentals=0
        ),
    )(source, *given)


def exchange(value, groups):
    rows, tokens = value.shape
    return lax.all_to_all(
        value.reshape(groups, rows // groups, tokens), "ctx", split_axis=0, concat_axis=0, tiled=True
    )


def on_device(
    mr_query, mr_key, mr_value, mr_filter, proj_weight, li_query, li_key, li_filter, li_skip
):
    rows, tokens = mr_key.shape
    half = tokens // 2
    groups = lax.axis_size("ctx")
    short = short_tables(tokens)
    tables = long_tables(groups, tokens)
    swap = [(0, 1), (1, 0)]
    mine = lax.axis_index("ch").astype(jnp.int32).reshape(1)

    late, border = short_conv(None, mr_key, mr_value, mr_query, mr_filter, short)
    border = lax.ppermute(border, "ctx", [(i, i + 1) for i in range(groups - 1)])
    other_late = lax.ppermute(late, "ch", swap)
    li_filter, late = lax.optimization_barrier((li_filter, late))
    filter_part = exchange(li_filter, groups)
    (early,) = short_conv(border, mr_key, mr_value, mr_query, mr_filter, short)
    other_early = lax.ppermute(early, "ch", swap)

    late_total, early_total = project_own(mine, proj_weight, late, early)
    li_input = project_other(1 - mine, proj_weight, other_late, late_total, li_key, 1)
    li_input = project_other(1 - mine, proj_weight, other_early, early_total, li_key, 0, li_input)

    direct = li_skip[:, None] * li_input.astype(F32)
    response, direct = lax.optimization_barrier((response_call(filter_part, tables), direct))
    long_part = convolve_call(exchange(li_input, groups), response, tables)
    long_local = exchange(long_part.reshape(rows, tokens), groups).reshape(rows, tokens)
    gated_out = li_query.astype(F32) * (long_local.astype(F32) + direct)
    return gated_out.astype(BF16)


def solution(mesh):
    in_specs = (
        P("ch", "ctx"),
        P("ch", "ctx"),
        P("ch", "ctx"),
        P("ch", None),
        P("ch", None),
        P("ch", "ctx"),
        P("ch", "ctx"),
        P("ch", "ctx"),
        P("ch"),
    )
    return jax.shard_map(
        on_device, mesh=mesh, in_specs=in_specs, out_specs=P("ch", "ctx"), check_vma=False
    )
```
